256 devices in a mesh: blk: 16 (over z, y_lo), dp: 16 (over x, y_hi, core).
Axes of the slice: x: 4, y: 4 (y_hi: 2, y_lo: 2; y = y_hi * 2 + y_lo), z: 8, core: 2. Of those that a mesh axis runs over, the one named last changes fastest.
Arguments:
- tokens: bfloat16 [65536, 2048], P(('blk', 'dp')), may hold values from -6 to 6
- cotangent: bfloat16 [65536, 2048], P(('blk', 'dp')), may hold values from -6 to 6
- combine_weights: bfloat16 [65536], P(('blk', 'dp')), may hold values from 0.19921875 to 1
- tile_expert: int32 [512], P(('blk', 'dp')), may hold values from 0 to 15, as said below
- tile_rows: int32 [512], P(('blk', 'dp')), may hold values from 64 to 128
- w_gate: bfloat16 [16, 2048, 768], P('blk', 'dp'), may hold values from -0.125 to 0.125
- w_up: bfloat16 [16, 2048, 768], P('blk', 'dp'), may hold values from -0.125 to 0.125
- w_down: bfloat16 [16, 2048, 768], P('blk', 'dp'), may hold values from -0.21875 to 0.21875
Outputs:
- merged: bfloat16 [65536, 2048], P(('blk', 'dp'))
- token_grad: bfloat16 [65536, 2048], P(('blk', 'dp'))
- grad_gate: float32 [16, 2048, 768], P('blk', 'dp')
- grad_up: float32 [16, 2048, 768], P('blk', 'dp')
- grad_down: float32 [16, 2048, 768], P('blk', 'dp')
The draws below stay inside these ranges and needn't reach their ends.
Inputs may be any that keep to these rules, and one draw needn't show every extreme that they name: `tile_expert`: expert e's weights sit on blk index e. On a device with blk index b, the first tile names expert b or (b - 1) mod 16, the last tile names b or (b + 1) mod 16, every other tile names b; both neighbours are named somewhere in every draw.
All inputs are finite; a program needn't handle non-finite values.
Results may differ from the reference program's by a relative error of at most 0.0057.
Values may be sent and summed in bfloat16 or wider, within the bound.
No kernel may reach another device: no remote copies, remote signals or barrier semaphores. Data moves between devices by JAX's collectives and lax.ppermute only.
A program may use at most 128 MiB of HBM per device.

```python
import math
import jax
import jax.numpy as jnp
from jax import lax

D = 2048
FH = 768
TILE = 128
TILES = 2
EXPERTS = 16
TOKENS = 65536


def draw_tile_expert(key, part):
    key = jax.random.fold_in(key, 11)
    tile_total = TOKENS // TILE
    position = jnp.arange(tile_total, dtype=jnp.int32)
    device = position // TILES
    per_owner = tile_total // (TILES * EXPERTS)
    owner_index = device // per_owner
    place_in_device = position % TILES
    coin_flip = jax.random.randint(key, (tile_total,), 0, 2).astype(jnp.int32)
    coin_flip = jnp.where(device == 0, 1, coin_flip)
    offset = jnp.where(place_in_device == 0, -coin_flip, jnp.where(place_in_device == TILES - 1, coin_flip, 0))
    return ((owner_index + offset + EXPERTS) % EXPERTS).astype(jnp.int32)


def draw_tile_rows(key, part):
    key = jax.random.fold_in(key, 23)
    tile_total = TOKENS // TILE
    counts = jax.random.randint(key, (tile_total,), TILE // 2, TILE + 1)
    return jnp.where(jnp.arange(tile_total) == 0, TILE, counts).astype(jnp.int32)


def block_levels(key, dims, cuts, smallest, high):
    def one(axis_at, parts):
        steps = jax.random.uniform(jax.random.fold_in(jax.random.fold_in(key, 6), axis_at), (parts,), jnp.float32, smallest / len(cuts), high / len(cuts))
        return jnp.repeat(jnp.exp(steps), dims[axis_at] // parts).reshape((-1,) + (1,) * (len(dims) - axis_at - 1))

    gain = one(*cuts[0])
    for cut in cuts[1:]:
        gain = gain * one(*cut)
    return gain


def normal_values(own_key, shape, scale, limit, split=(), kind=jnp.bfloat16):
    result = jax.random.normal(own_key, shape, jnp.float32) * scale
    if len(split) > 0:
        result = block_levels(own_key, shape, split, -0.22, 0.18) * result
    return jnp.clip(result, min=-limit, max=limit).astype(kind)


def setup_inputs(seed: int = 0) -> dict:
    arg_keys = jax.random.split(jax.random.key(seed), 9)
    tokens = normal_values(arg_keys[0], (TOKENS, D), 1.0, 6.0, ((0, 256),))
    cotangent = normal_values(arg_keys[1], (TOKENS, D), 1.0, 6.0, ((0, 256),))
    combine_weights = jnp.clip(jnp.exp(math.log(1.0) - 1.6133518 * jax.random.uniform(arg_keys[2], (TOKENS,), jnp.float32) ** block_levels(arg_keys[2], (TOKENS,), ((0, 256),), -0.2, 0.2)), 0.19921875, 1.0).astype(jnp.bfloat16)
    tile_expert = draw_tile_expert(jax.random.fold_in(arg_keys[8], 71), 0)
    tile_rows = draw_tile_rows(jax.random.fold_in(arg_keys[8], 71), 0)
    w_gate = normal_values(arg_keys[5], (EXPERTS, D, FH), D ** -0.5, 0.125, ((0, 16), (1, 16)))
    w_up = normal_values(arg_keys[6], (EXPERTS, D, FH), D ** -0.5, 0.125, ((0, 16), (1, 16)))
    w_down = normal_values(arg_keys[7], (EXPERTS, D, FH), FH ** -0.5, 0.21875, ((0, 16), (1, 16)))
    return {"tokens": tokens, "cotangent": cotangent, "combine_weights": combine_weights, "tile_expert": tile_expert, "tile_rows": tile_rows, "w_gate": w_gate, "w_up": w_up, "w_down": w_down}


def forward_rows(row_block, scales, gate_full, up_full, down_full):
    gate_pre = jnp.dot(row_block, gate_full, preferred_element_type=jnp.float32)
    up_pre = jnp.dot(row_block, up_full, preferred_element_type=jnp.float32)
    sigmoid_gate = jax.nn.sigmoid(gate_pre)
    activated = gate_pre * sigmoid_gate
    hidden = (activated * up_pre).astype(jnp.bfloat16)
    projected = lax.dot_general(hidden, down_full, (((1,), (1,)), ((), ())), preferred_element_type=jnp.float32)
    output = (scales.astype(jnp.float32)[:, None] * projected).astype(jnp.bfloat16)
    return (output, (gate_pre, up_pre, sigmoid_gate, activated, hidden))

def scaled_grad(cotangent, scales):
    return (scales.astype(jnp.float32)[:, None] * cotangent.astype(jnp.float32)).astype(jnp.bfloat16)

def backward_rows(grad_block, saved, gate_full, up_full, down_full):
    gate_pre, up_pre, sigmoid_gate, activated, hidden = saved
    hidden_grad = jnp.dot(grad_block, down_full, preferred_element_type=jnp.float32)
    gate_grad = (hidden_grad * up_pre * sigmoid_gate * (1.0 + gate_pre * (1.0 - sigmoid_gate))).astype(jnp.bfloat16)
    up_grad = (hidden_grad * activated).astype(jnp.bfloat16)
    contract = (((1,), (1,)), ((), ()))
    input_grad = lax.dot_general(gate_grad, gate_full, contract, preferred_element_type=jnp.float32)
    input_grad = input_grad + lax.dot_general(up_grad, up_full, contract, preferred_element_type=jnp.float32)
    return (input_grad.astype(jnp.bfloat16), gate_grad, up_grad)

def reference(tokens, cotangent, combine_weights, tile_expert, tile_rows, w_gate, w_up, w_down):
    tile_total = tile_expert.shape[0]
    tile_len = tokens.shape[0] // tile_total
    width = tokens.shape[1]
    live_rows = lax.broadcasted_iota(jnp.int32, (tile_total, tile_len), 1) < tile_rows[:, None]
    scaled = jnp.where(live_rows, combine_weights.reshape(tile_total, tile_len), jnp.zeros((), combine_weights.dtype))
    outer = (((0,), (0,)), ((), ()))

    def tile_step(totals, inputs_now):
        tile_tokens, tile_cot, tile_scales, expert = inputs_now
        gate_full = w_gate[expert]
        up_full = w_up[expert]
        down_full = w_down[expert]
        output, saved = forward_rows(tile_tokens, tile_scales, gate_full, up_full, down_full)
        grad_block = scaled_grad(tile_cot, tile_scales)
        input_grad, gate_grad, up_grad = backward_rows(grad_block, saved, gate_full, up_full, down_full)
        gate_total = lax.dot_general(tile_tokens, gate_grad, outer, preferred_element_type=jnp.float32)
        up_total = lax.dot_general(tile_tokens, up_grad, outer, preferred_element_type=jnp.float32)
        down_total = lax.dot_general(grad_block, saved[4], outer, preferred_element_type=jnp.float32)
        totals = (totals[0].at[expert].add(gate_total), totals[1].at[expert].add(up_total), totals[2].at[expert].add(down_total))
        return (totals, (output, input_grad))
    start = (jnp.zeros(w_gate.shape, jnp.float32), jnp.zeros(w_gate.shape, jnp.float32), jnp.zeros(w_gate.shape, jnp.float32))
    totals, results = lax.scan(tile_step, start, (tokens.reshape(tile_total, tile_len, width), cotangent.reshape(tile_total, tile_len, width), scaled, tile_expert))
    return (results[0].reshape(tokens.shape), results[1].reshape(tokens.shape), totals[0], totals[1], totals[2])
```

```python
import jax
import jax.numpy as jnp
from jax import lax
from jax.sharding import PartitionSpec as P

BF = jnp.bfloat16
F32 = jnp.float32
Z, YL, X, YH, C = 8, 2, 4, 2, 2


def move(value, to):
    pairs = []
    for source in range(Z * YL * X * YH * C):
        rest, c = divmod(source, C)
        rest, yh = divmod(rest, YH)
        rest, x = divmod(rest, X)
        z, yl = divmod(rest, YL)
        z, yl, x, yh, c = to(z, yl, x, yh, c)
        target = ((((z % Z) * YL + yl % YL) * X + x % X) * YH + yh % YH) * C + c % C
        pairs.append((source, target))
    return lax.ppermute(value, ("blk", "dp"), pairs)


def x_up(value):
    return move(value, lambda z, yl, x, yh, c: (z, yl, x + 1, yh, c))


def x_down(value):
    return move(value, lambda z, yl, x, yh, c: (z, yl, x - 1, yh, c))


def yh_swap(value):
    return move(value, lambda z, yl, x, yh, c: (z, yl, x, yh + 1, c))


def core_swap(value):
    return move(value, lambda z, yl, x, yh, c: (z, yl, x, yh, c + 1))


def blk_up(value):
    def to(z, yl, x, yh, c):
        y = (yh * YL + yl + 1) % (YH * YL)
        return z + yl, y % YL, x, y // YL, c

    return move(value, to)


def blk_down(value):
    def to(z, yl, x, yh, c):
        y = (yh * YL + yl - 1) % (YH * YL)
        return z - (1 - yl), y % YL, x, y // YL, c

    return move(value, to)


def dot(a, b, ca, cb):
    return lax.dot_general(a, b, (((ca,), (cb,)), ((), ())), preferred_element_type=F32)


def shards(tokens, cotangent, combine_weights, tile_expert, tile_rows, w_gate, w_up, w_down):
    count = lax.axis_size("blk")
    blk = lax.axis_index("blk")
    dp = lax.axis_index("dp")
    x, yh, c = dp // (YH * C), (dp // C) % YH, dp % C
    piece, hidden = w_gate.shape[1], w_gate.shape[2]
    local, width = tokens.shape
    tiles = tile_expert.shape[0]
    tile = local // tiles
    nothing = jnp.zeros((), BF)

    own = jnp.concatenate([w_gate[0], w_up[0], w_down[0]], axis=1)
    other = yh_swap(own)
    left_own, right_own = x_up(own), x_down(own)
    left_other, right_other = x_up(other), x_down(other)
    far_own, far_other = x_up(left_own), x_down(right_other)
    near = {
        0: jnp.concatenate([own, other], axis=0),
        1: jnp.concatenate([right_own, right_other], axis=0),
        2: jnp.concatenate([far_own, far_other], axis=0),
        3: jnp.concatenate([left_own, left_other], axis=0),
    }

    stay = tile_expert == blk
    live = lax.broadcasted_iota(jnp.int32, (tiles, tile), 1) < tile_rows[:, None]
    scales = jnp.where(live, combine_weights.reshape(tiles, tile), nothing)
    own_scales = jnp.where(stay[:, None], scales, nothing)
    away_scales = jnp.where(stay[:, None], nothing, scales)
    tok = tokens.reshape(tiles, tile, width)
    cot = cotangent.reshape(tiles, tile, width)

    def scaled(values, by):
        return (by.astype(F32)[:, None] * values.astype(F32)).astype(BF)

    def parcel(at):
        note = jnp.pad(away_scales[at][None], ((0, 15), (0, width - tile)))
        return jnp.concatenate([tok[at], scaled(cot[at], away_scales[at]), note], axis=0)

    def opened(box):
        return box[:tile], box[tile : 2 * tile], box[2 * tile, :tile]

    lower = opened(blk_up(parcel(tiles - 1)))
    upper = opened(blk_down(parcel(0)))
    rows = jnp.concatenate([tokens, lower[0], upper[0]], axis=0)
    scaled_cot = jnp.concatenate(
        [scaled(cotangent, own_scales.reshape(local)), lower[1], upper[1]], axis=0
    )
    all_scales = jnp.concatenate([own_scales.reshape(local), lower[2], upper[2]], axis=0)

    def place(r, cr, yr):
        return (((x + r) % X) * YH + (yh + yr) % YH) * C + (c + cr) % C

    def columns(values, r):
        return jnp.concatenate(
            [
                lax.dynamic_slice_in_dim(values, place(r, cr, yr) * piece, piece, axis=1)
                for cr in range(C)
                for yr in range(YH)
            ],
            axis=1,
        )

    order = (0, 3, 1, 2)
    rows_by = {r: columns(rows, r) for r in order}
    cot_by = {r: columns(scaled_cot, r) for r in order}
    weights = {r: jnp.concatenate([near[r], core_swap(near[r])], axis=0) for r in order}
    gate_up = sum(dot(rows_by[r], weights[r][:, : 2 * hidden], 1, 0) for r in order)
    hidden_grad = sum(dot(cot_by[r], weights[r][:, 2 * hidden :], 1, 0) for r in order)
    gate_pre, up_pre = gate_up[:, :hidden], gate_up[:, hidden:]
    sig = jax.nn.sigmoid(gate_pre)
    act = gate_pre * sig
    hid = (act * up_pre).astype(BF)
    gate_grad = (hidden_grad * up_pre * sig * (1.0 + gate_pre * (1.0 - sig))).astype(BF)
    up_grad = (hidden_grad * act).astype(BF)
    both_grad = jnp.concatenate([gate_grad, up_grad], axis=1)

    half = YH * piece
    keep, swapped = {}, {}
    for r in (2, 1, 3, 0):
        part = jnp.concatenate(
            [dot(rows_by[r], both_grad, 0, 0), dot(cot_by[r], hid, 0, 0)], axis=1
        )
        keep[r] = part[:half] + core_swap(part[half:].astype(BF)).astype(F32)
    far_a = x_up(keep[2][:piece].astype(BF))
    far_b = x_down(keep[2][piece:].astype(BF))
    one_b = x_up(keep[1][piece:].astype(BF))
    one_a = x_down(keep[3][:piece].astype(BF))
    two_a = x_up((keep[1][:piece] + far_a.astype(F32)).astype(BF))
    two_b = x_down((keep[3][piece:] + far_b.astype(F32)).astype(BF))
    mine = keep[0][:piece] + one_a.astype(F32) + two_a.astype(F32)
    theirs = keep[0][piece:] + one_b.astype(F32) + two_b.astype(F32)
    grads = mine + yh_swap(theirs.astype(BF)).astype(F32)

    whole = jnp.zeros((X * YH * C * piece, 3 * hidden), BF)
    for r in order:
        for cr in range(C):
            for yr in range(YH):
                at = (cr * YH + yr) * piece
                whole = lax.dynamic_update_slice_in_dim(
                    whole, weights[r][at : at + piece], place(r, cr, yr) * piece, axis=0
                )
    input_grad = dot(both_grad, whole[:, : 2 * hidden], 1, 1).astype(BF)
    output = (all_scales.astype(F32)[:, None] * dot(hid, whole[:, 2 * hidden :], 1, 1)).astype(BF)

    def box(at):
        return jnp.concatenate([output[at : at + tile], input_grad[at : at + tile]], axis=0)

    back_last = blk_down(box(local))
    back_first = blk_up(box(local + tile))

    def settled(values, first, last):
        return jnp.concatenate(
            [
                jnp.where(stay[0], values[:tile], first),
                values[tile : local - tile],
                jnp.where(stay[tiles - 1], values[local - tile : local], last),
            ],
            axis=0,
        )

    merged = settled(output, back_first[:tile], back_last[:tile])
    token_grad = settled(input_grad, back_first[tile:], back_last[tile:])
    return (
        merged,
        token_grad,
        grads[None, :, :hidden],
        grads[None, :, hidden : 2 * hidden],
        grads[None, :, 2 * hidden :],
    )


def solution(mesh):
    flat = P(("blk", "dp"))
    weight = P("blk", "dp", None)
    wide = P(("blk", "dp"), None)
    in_specs = (wide, wide, flat, flat, flat, weight, weight, weight)
    out_specs = (wide, wide, weight, weight, weight)
    return jax.shard_map(shards, mesh=mesh, in_specs=in_specs, out_specs=out_specs, check_vma=False)
```

```python
import jax
import jax.numpy as jnp
from jax import lax
from jax.experimental import pallas as pl
from jax.experimental.pallas import tpu as pltpu
from jax.sharding import PartitionSpec as P

BF = jnp.bfloat16
F32 = jnp.float32
Z, YL, X, YH, C = 8, 2, 4, 2, 2


def move(value, to):
    pairs = []
    for source in range(Z * YL * X * YH * C):
        rest, c = divmod(source, C)
        rest, yh = divmod(rest, YH)
        rest, x = divmod(rest, X)
        z, yl = divmod(rest, YL)
        z, yl, x, yh, c = to(z, yl, x, yh, c)
        target = ((((z % Z) * YL + yl % YL) * X + x % X) * YH + yh % YH) * C + c % C
        pairs.append((source, target))
    return lax.ppermute(value, ("blk", "dp"), pairs)


def x_up(value):
    return move(value, lambda z, yl, x, yh, c: (z, yl, x + 1, yh, c))


def x_down(value):
    return move(value, lambda z, yl, x, yh, c: (z, yl, x - 1, yh, c))


def yh_swap(value):
    return move(value, lambda z, yl, x, yh, c: (z, yl, x, yh + 1, c))


def core_swap(value):
    return move(value, lambda z, yl, x, yh, c: (z, yl, x, yh, c + 1))


def blk_up(value):
    def to(z, yl, x, yh, c):
        y = (yh * YL + yl + 1) % (YH * YL)
        return z + yl, y % YL, x, y // YL, c

    return move(value, to)


def blk_down(value):
    def to(z, yl, x, yh, c):
        y = (yh * YL + yl - 1) % (YH * YL)
        return z - (1 - yl), y % YL, x, y // YL, c

    return move(value, to)


def dot(a, b, ca, cb):
    return lax.dot_general(a, b, (((ca,), (cb,)), ((), ())), preferred_element_type=F32)


def after(values, *others):
    return lax.optimization_barrier((values, others))[0]


def together(*values):
    return lax.optimization_barrier(values)


def local_kernel(body, out_shape, operands, in_smem):
    specs = [
        pl.BlockSpec(memory_space=pltpu.SMEM if i < in_smem else pltpu.VMEM)
        for i in range(len(operands))
    ]
    return pl.pallas_call(
        body,
        out_shape=out_shape,
        in_specs=specs,
        out_specs=[pl.BlockSpec(memory_space=pltpu.VMEM)] * len(out_shape),
        compiler_params=pltpu.CompilerParams(vmem_limit_bytes=40 * 2**20),
        cost_estimate=pl.CostEstimate(flops=0, bytes_accessed=0, transcendentals=0),
    )(*operands)


def by_distance(places, groups, tile):
    arrays, spans = [], []
    for group in groups:
        spans.append([])
        for array, first in group:
            if not any(array is a for a in arrays):
                arrays.append(array)
            at = next(i for i, a in enumerate(arrays) if a is array)
            spans[-1].append((at, first))
    width = arrays[0].shape[1]
    block = width // places.shape[0]

    def body(place_ref, *refs):
        sources, outs = refs[: len(arrays)], refs[len(arrays) :]
        for i in range(places.shape[0]):
            column = pl.multiple_of(place_ref[i] * block, block)
            for out, span in zip(outs, spans):
                for k, (at, first) in enumerate(span):
                    out[k * tile : (k + 1) * tile, i * block : (i + 1) * block] = sources[at][
                        first : first + tile, pl.ds(column, block)
                    ]

    shapes = [jax.ShapeDtypeStruct((len(span) * tile, width), BF) for span in spans]
    return local_kernel(body, shapes, (places, *arrays), 1)


def weight_grads(rows, cots, both_grad, hid, first, step, count):
    length, width = rows.shape
    each, half = width // X, width // X // C
    hidden = hid.shape[1]
    lefts = (((0,), (0,)), ((), ()))

    def body(rows_ref, cots_ref, grad_ref, hid_ref, send_ref, keep_ref):
        for cr, out in ((1, send_ref), (0, keep_ref)):
            at = slice(cr * half, (cr + 1) * half)
            part = lax.dot_general(
                rows_ref[:, at], grad_ref[...], lefts, preferred_element_type=F32
            )
            out[:, : 2 * hidden] = part.astype(out.dtype)
            part = lax.dot_general(
                cots_ref[:, at], hid_ref[...], lefts, preferred_element_type=F32
            )
            out[:, 2 * hidden :] = part.astype(out.dtype)

    column = pl.BlockSpec((length, each), lambda i: (0, first + i * step))
    result = pl.BlockSpec((half, 3 * hidden), lambda i: (i, 0))
    shape = (count * half, 3 * hidden)
    return pl.pallas_call(
        body,
        grid=(count,),
        out_shape=[jax.ShapeDtypeStruct(shape, BF), jax.ShapeDtypeStruct(shape, F32)],
        in_specs=[
            column,
            column,
            pl.BlockSpec(both_grad.shape, lambda i: (0, 0)),
            pl.BlockSpec(hid.shape, lambda i: (0, 0)),
        ],
        out_specs=[result, result],
        compiler_params=pltpu.CompilerParams(vmem_limit_bytes=32 * 2**20),
        cost_estimate=pl.CostEstimate(flops=0, bytes_accessed=0, transcendentals=0),
    )(rows, cots, both_grad, hid)


def outputs_by_column(places, hid, both_grad, scales, weights, local, tile):
    count = len(weights)
    each, hidden = weights[0].shape[0], hid.shape[1]
    block = each // YH
    width = block * places.shape[0]
    rights = (((1,), (1,)), ((), ()))

    def body(place_ref, hid_ref, grad_ref, scale_ref, *refs):
        own_out, own_grad, last, first = refs[count:]
        for k in range(count // C):
            for yr in range(YH):
                pair = [refs[k * C + cr] for cr in range(C)]
                at = slice(yr * block, (yr + 1) * block)
                wide = slice(0, 2 * hidden)
                down = slice(2 * hidden, 3 * hidden)
                both = jnp.concatenate([ref[at, wide] for ref in pair], axis=0)
                grad = lax.dot_general(grad_ref[...], both, rights, preferred_element_type=F32)
                grad = grad.astype(BF)
                both = jnp.concatenate([ref[at, down] for ref in pair], axis=0)
                out = lax.dot_general(hid_ref[...], both, rights, preferred_element_type=F32)
                out = (scale_ref[...] * out).astype(BF)
                for cr in range(C):
                    column = place_ref[(k * C + cr) * YH + yr] * block
                    to = pl.ds(pl.multiple_of(column, block), block)
                    part = slice(cr * block, (cr + 1) * block)
                    own_out[:, to] = out[:local, part]
                    own_grad[:, to] = grad[:local, part]
                    for box, row in ((last, local), (first, local + tile)):
                        box[:tile, to] = out[row : row + tile, part]
                        box[tile:, to] = grad[row : row + tile, part]

    own = jax.ShapeDtypeStruct((local, width), BF)
    box = jax.ShapeDtypeStruct((2 * tile, width), BF)
    return local_kernel(
        body, [own, own, box, box], (places, hid, both_grad, scales, *weights), 1
    )


def settled(stay, own_out, own_grad, first, last, tile):
    local = own_out.shape[0]

    def body(stay_ref, own_out_ref, own_grad_ref, first_ref, last_ref, out_ref, grad_ref):
        for own, out, row in ((own_out_ref, out_ref, 0), (own_grad_ref, grad_ref, tile)):
            out[...] = own[...]
            for k, box in ((0, first_ref), (local // tile - 1, last_ref)):

                @pl.when(stay_ref[k] == 0)
                def _(out=out, box=box, k=k, row=row):
                    out[k * tile : (k + 1) * tile, :] = box[row : row + tile, :]

    shape = jax.ShapeDtypeStruct(own_out.shape, BF)
    return local_kernel(body, [shape, shape], (stay, own_out, own_grad, first, last), 1)


def shards(tokens, cotangent, combine_weights, tile_expert, tile_rows, w_gate, w_up, w_down):
    count = lax.axis_size("blk")
    blk = lax.axis_index("blk")
    dp = lax.axis_index("dp")
    x, yh, c = dp // (YH * C), (dp // C) % YH, dp % C
    piece, hidden = w_gate.shape[1], w_gate.shape[2]
    local, width = tokens.shape
    tiles = tile_expert.shape[0]
    tile = local // tiles
    nothing = jnp.zeros((), BF)

    own = jnp.concatenate([w_gate[0], w_up[0], w_down[0]], axis=1)
    other = yh_swap(own)
    left_own, right_own = x_up(own), x_down(own)
    other, left_own, right_own = together(other, left_own, right_own)
    left_other, right_other = x_up(other), x_down(other)
    near, across = {}, {}
    near[0] = jnp.concatenate([own, other], axis=0)
    across[0] = core_swap(near[0])

    stay = tile_expert == blk
    live = lax.broadcasted_iota(jnp.int32, (tiles, tile), 1) < tile_rows[:, None]
    scales = jnp.where(live, combine_weights.reshape(tiles, tile), nothing)
    own_scales = jnp.where(stay[:, None], scales, nothing)
    away_scales = jnp.where(stay[:, None], nothing, scales)
    tok = tokens.reshape(tiles, tile, width)
    cot = cotangent.reshape(tiles, tile, width)

    def scaled(values, by):
        return (by.astype(F32)[:, None] * values.astype(F32)).astype(BF)

    def parcel(at):
        note = jnp.pad(away_scales[at][None], ((0, 15), (0, width - tile)))
        return jnp.concatenate([tok[at], scaled(cot[at], away_scales[at]), note], axis=0)

    up_parcel, down_parcel = after((parcel(tiles - 1), parcel(0)), other)
    left_other, right_other = together(left_other, right_other)
    near[3] = jnp.concatenate([left_own, left_other], axis=0)
    near[1] = jnp.concatenate([right_own, right_other], axis=0)
    own_cot = scaled(cotangent, own_scales.reshape(local))
    places = jnp.stack(
        [
            (((x + r) % X) * YH + (yh + yr) % YH) * C + (c + cr) % C
            for r in range(X)
            for cr in range(C)
            for yr in range(YH)
        ]
    ).astype(jnp.int32)
    own_at = [k * tile for k in range(tiles)]
    rows_own, cot_own = by_distance(
        places, ([(tokens, k) for k in own_at], [(own_cot, k) for k in own_at]), tile
    )
    across[3] = core_swap(near[3])
    across[1] = core_swap(after(near[1], across[3]))
    half = YH * piece

    def span(r, cr):
        return slice((r * C + cr) * half, (r * C + cr + 1) * half)

    def projected(rows, cots, r, cr):
        weight = (across if cr else near)[r]
        return (
            dot(rows[:, span(r, cr)], weight[:, : 2 * hidden], 1, 0),
            dot(cots[:, span(r, cr)], weight[:, 2 * hidden :], 1, 0),
        )

    def total(rows, cots, group):
        parts = [projected(rows, cots, r, cr) for r in group for cr in range(C)]
        return sum(p[0] for p in parts), sum(p[1] for p in parts)

    early = total(rows_own, cot_own, (0, 3, 1))
    far_own, far_other, lower, upper, early = together(
        x_up(after(left_own, left_other)),
        x_down(right_other),
        blk_up(up_parcel),
        blk_down(down_parcel),
        early,
    )
    all_scales = jnp.concatenate(
        [own_scales.reshape(local), lower[2 * tile, :tile], upper[2 * tile, :tile]], axis=0
    )
    rows_vis, cot_vis = by_distance(
        places, ([(lower, 0), (upper, 0)], [(lower, tile), (upper, tile)]), tile
    )
    near[2] = jnp.concatenate([far_own, far_other], axis=0)
    across[2] = core_swap(near[2])
    early_vis = total(rows_vis, cot_vis, (0, 3, 1))
    stack = lambda a, b: jnp.concatenate([a, b], axis=0)
    rows, cots = stack(rows_own, rows_vis), stack(cot_own, cot_vis)
    late = total(rows, cots, (2,))
    gate_up = stack(early[0], early_vis[0]) + late[0]
    hidden_grad = stack(early[1], early_vis[1]) + late[1]
    gate_pre, up_pre = gate_up[:, :hidden], gate_up[:, hidden:]
    sig = jax.nn.sigmoid(gate_pre)
    act = gate_pre * sig
    hid = (act * up_pre).astype(BF)
    gate_grad = (hidden_grad * up_pre * sig * (1.0 + gate_pre * (1.0 - sig))).astype(BF)
    up_grad = (hidden_grad * act).astype(BF)
    both_grad = jnp.concatenate([gate_grad, up_grad], axis=1)

    keep = {}

    def paired(first, step, count, *before):
        grad, act_hid = after((both_grad, hid), *before)
        sends, keeps = weight_grads(rows, cots, grad, act_hid, first, step, count)
        came = core_swap(sends)
        for i in range(count):
            at = slice(i * half, (i + 1) * half)
            keep[(first + i * step) % X] = keeps[at] + came[at].astype(F32)
        return came

    paired(2, 1, 1)
    near_a, near_b = together(keep[2][:piece].astype(BF), keep[2][piece:].astype(BF))
    far_a, far_b = x_up(near_a), x_down(near_b)
    came = paired(1, 2, 2, near_a, near_b)

    late_hid, late_grad = after((hid, both_grad), came)
    weights = [w for r in range(X) for w in (near[r], across[r])]
    own_out, own_grad, box_last, box_first = outputs_by_column(
        places, late_hid, late_grad, all_scales.astype(F32)[:, None], weights, local, tile
    )

    far_a, far_b, box_last, box_first = together(far_a, far_b, box_last, box_first)
    step_up = jnp.concatenate(
        [(keep[1][:piece] + far_a.astype(F32)).astype(BF), keep[1][piece:].astype(BF)], axis=0
    )
    step_down = jnp.concatenate(
        [keep[3][:piece].astype(BF), (keep[3][piece:] + far_b.astype(F32)).astype(BF)], axis=0
    )
    come_up, come_down = x_up(step_up), x_down(step_down)
    back_last, back_first = blk_down(box_last), blk_up(box_first)
    paired(0, 1, 1, box_last, box_first)
    summed = keep[0] + come_up.astype(F32) + come_down.astype(F32)
    grads = summed[:piece] + yh_swap(summed[piece:].astype(BF)).astype(F32)
    merged, token_grad = settled(
        stay.astype(jnp.int32), own_out, own_grad, back_first, back_last, tile
    )
    return (
        merged,
        token_grad,
        grads[None, :, :hidden],
        grads[None, :, hidden : 2 * hidden],
        grads[None, :, 2 * hidden :],
    )


def solution(mesh):
    flat = P(("blk", "dp"))
    weight = P("blk", "dp", None)
    wide = P(("blk", "dp"), None)
    in_specs = (wide, wide, flat, flat, flat, weight, weight, weight)
    out_specs = (wide, wide, weight, weight, weight)
    return jax.shard_map(shards, mesh=mesh, in_specs=in_specs, out_specs=out_specs, check_vma=False)
```

```python
import jax
import jax.numpy as jnp
from jax import lax
from jax.experimental import pallas as pl
from jax.experimental.pallas import tpu as pltpu
from jax.sharding import PartitionSpec as P

BF = jnp.bfloat16
F32 = jnp.float32
Z, YL, X, YH, C = 8, 2, 4, 2, 2


def move(value, to):
    pairs = []
    for source in range(Z * YL * X * YH * C):
        rest, c = divmod(source, C)
        rest, yh = divmod(rest, YH)
        rest, x = divmod(rest, X)
        z, yl = divmod(rest, YL)
        z, yl, x, yh, c = to(z, yl, x, yh, c)
        target = ((((z % Z) * YL + yl % YL) * X + x % X) * YH + yh % YH) * C + c % C
        pairs.append((source, target))
    return lax.ppermute(value, ("blk", "dp"), pairs)


def x_up(value):
    return move(value, lambda z, yl, x, yh, c: (z, yl, x + 1, yh, c))


def x_down(value):
    return move(value, lambda z, yl, x, yh, c: (z, yl, x - 1, yh, c))


def yh_swap(value):
    return move(value, lambda z, yl, x, yh, c: (z, yl, x, yh + 1, c))


def core_swap(value):
    return move(value, lambda z, yl, x, yh, c: (z, yl, x, yh, c + 1))


def blk_up(value):
    def to(z, yl, x, yh, c):
        y = (yh * YL + yl + 1) % (YH * YL)
        return z + yl, y % YL, x, y // YL, c

    return move(value, to)


def blk_down(value):
    def to(z, yl, x, yh, c):
        y = (yh * YL + yl - 1) % (YH * YL)
        return z - (1 - yl), y % YL, x, y // YL, c

    return move(value, to)


def dot(a, b, ca, cb):
    return lax.dot_general(a, b, (((ca,), (cb,)), ((), ())), preferred_element_type=F32)


def after(values, *others):
    return lax.optimization_barrier((values, others))[0]


def together(*values):
    return lax.optimization_barrier(values)


def local_kernel(body, out_shape, operands, in_smem, mib=40):
    specs = [
        pl.BlockSpec(memory_space=pltpu.SMEM if i < in_smem else pltpu.VMEM)
        for i in range(len(operands))
    ]
    return pl.pallas_call(
        body,
        out_shape=out_shape,
        in_specs=specs,
        out_specs=[pl.BlockSpec(memory_space=pltpu.VMEM)] * len(out_shape),
        compiler_params=pltpu.CompilerParams(vmem_limit_bytes=mib * 2**20),
        cost_estimate=pl.CostEstimate(flops=0, bytes_accessed=0, transcendentals=0),
    )(*operands)


def by_distance(places, groups, tile):
    arrays, spans = [], []
    for group in groups:
        spans.append([])
        for array, first in group:
            if not any(array is a for a in arrays):
                arrays.append(array)
            at = next(i for i, a in enumerate(arrays) if a is array)
            spans[-1].append((at, first))
    width = arrays[0].shape[1]
    block = width // places.shape[0]

    def body(place_ref, *refs):
        sources, outs = refs[: len(arrays)], refs[len(arrays) :]
        for i in range(places.shape[0]):
            column = pl.multiple_of(place_ref[i] * block, block)
            for out, span in zip(outs, spans):
                for k, (at, first) in enumerate(span):
                    out[k * tile : (k + 1) * tile, i * block : (i + 1) * block] = sources[at][
                        first : first + tile, pl.ds(column, block)
                    ]

    shapes = [jax.ShapeDtypeStruct((len(span) * tile, width), BF) for span in spans]
    return local_kernel(body, shapes, (places, *arrays), 1)


def weight_grads(rows, cots, both_grad, hid, first, step, count):
    length, width = rows.shape
    each, half = width // X, width // X // C
    hidden = hid.shape[1]
    lefts = (((0,), (0,)), ((), ()))

    def body(rows_ref, cots_ref, grad_ref, hid_ref, send_ref, keep_ref):
        for cr, out in ((1, send_ref), (0, keep_ref)):
            at = slice(cr * half, (cr + 1) * half)
            part = lax.dot_general(
                rows_ref[:, at], grad_ref[...], lefts, preferred_element_type=F32
            )
            out[:, : 2 * hidden] = part.astype(out.dtype)
            part = lax.dot_general(
                cots_ref[:, at], hid_ref[...], lefts, preferred_element_type=F32
            )
            out[:, 2 * hidden :] = part.astype(out.dtype)

    column = pl.BlockSpec((length, each), lambda i: (0, first + i * step))
    result = pl.BlockSpec((half, 3 * hidden), lambda i: (i, 0))
    shape = (count * half, 3 * hidden)
    return pl.pallas_call(
        body,
        grid=(count,),
        out_shape=[jax.ShapeDtypeStruct(shape, BF), jax.ShapeDtypeStruct(shape, F32)],
        in_specs=[
            column,
            column,
            pl.BlockSpec(both_grad.shape, lambda i: (0, 0)),
            pl.BlockSpec(hid.shape, lambda i: (0, 0)),
        ],
        out_specs=[result, result],
        compiler_params=pltpu.CompilerParams(vmem_limit_bytes=32 * 2**20),
        cost_estimate=pl.CostEstimate(flops=0, bytes_accessed=0, transcendentals=0),
    )(rows, cots, both_grad, hid)


def outputs_by_column(places, hid, both_grad, scales, weights, local, tile):
    count = len(weights)
    each, hidden = weights[0].shape[0], hid.shape[1]
    block = each // YH
    width = block * places.shape[0]
    rights = (((1,), (1,)), ((), ()))

    def body(place_ref, hid_ref, grad_ref, scale_ref, *refs):
        own_out, own_grad, last, first = refs[count:]
        for k in range(count // C):
            for yr in range(YH):
                pair = [refs[k * C + cr] for cr in range(C)]
                at = slice(yr * block, (yr + 1) * block)
                wide = slice(0, 2 * hidden)
                down = slice(2 * hidden, 3 * hidden)
                both = jnp.concatenate([ref[at, wide] for ref in pair], axis=0)
                grad = lax.dot_general(grad_ref[...], both, rights, preferred_element_type=F32)
                grad = grad.astype(BF)
                both = jnp.concatenate([ref[at, down] for ref in pair], axis=0)
                out = lax.dot_general(hid_ref[...], both, rights, preferred_element_type=F32)
                out = (scale_ref[...] * out).astype(BF)
                for cr in range(C):
                    column = place_ref[(k * C + cr) * YH + yr] * block
                    to = pl.ds(pl.multiple_of(column, block), block)
                    part = slice(cr * block, (cr + 1) * block)
                    own_out[:, to] = out[:local, part]
                    own_grad[:, to] = grad[:local, part]
                    for box, row in ((last, local), (first, local + tile)):
                        box[:tile, to] = out[row : row + tile, part]
                        box[tile:, to] = grad[row : row + tile, part]

    own = jax.ShapeDtypeStruct((local, width), BF)
    box = jax.ShapeDtypeStruct((2 * tile, width), BF)
    return local_kernel(
        body, [own, own, box, box], (places, hid, both_grad, scales, *weights), 1, 58
    )


def settled(stay, own_out, own_grad, first, last, tile):
    local = own_out.shape[0]

    def body(stay_ref, own_out_ref, own_grad_ref, first_ref, last_ref, out_ref, grad_ref):
        for own, out, row in ((own_out_ref, out_ref, 0), (own_grad_ref, grad_ref, tile)):
            out[...] = own[...]
            for k, box in ((0, first_ref), (local // tile - 1, last_ref)):

                @pl.when(stay_ref[k] == 0)
                def _(out=out, box=box, k=k, row=row):
                    out[k * tile : (k + 1) * tile, :] = box[row : row + tile, :]

    shape = jax.ShapeDtypeStruct(own_out.shape, BF)
    return local_kernel(body, [shape, shape], (stay, own_out, own_grad, first, last), 1)


def shards(tokens, cotangent, combine_weights, tile_expert, tile_rows, w_gate, w_up, w_down):
    count = lax.axis_size("blk")
    blk = lax.axis_index("blk")
    dp = lax.axis_index("dp")
    x, yh, c = dp // (YH * C), (dp // C) % YH, dp % C
    piece, hidden = w_gate.shape[1], w_gate.shape[2]
    local, width = tokens.shape
    tiles = tile_expert.shape[0]
    tile = local // tiles
    nothing = jnp.zeros((), BF)

    own = jnp.concatenate([w_gate[0], w_up[0], w_down[0]], axis=1)
    other = yh_swap(own)
    left_own, right_own = x_up(own), x_down(own)
    other, left_own, right_own = together(other, left_own, right_own)
    left_other, right_other = x_up(other), x_down(other)
    near, across = {}, {}
    near[0] = jnp.concatenate([own, other], axis=0)
    across[0] = core_swap(near[0])

    stay = tile_expert == blk
    live = lax.broadcasted_iota(jnp.int32, (tiles, tile), 1) < tile_rows[:, None]
    scales = jnp.where(live, combine_weights.reshape(tiles, tile), nothing)
    own_scales = jnp.where(stay[:, None], scales, nothing)
    away_scales = jnp.where(stay[:, None], nothing, scales)
    tok = tokens.reshape(tiles, tile, width)
    cot = cotangent.reshape(tiles, tile, width)

    def scaled(values, by):
        return (by.astype(F32)[:, None] * values.astype(F32)).astype(BF)

    def parcel(at):
        note = jnp.pad(away_scales[at][None], ((0, 15), (0, width - tile)))
        return jnp.concatenate([tok[at], scaled(cot[at], away_scales[at]), note], axis=0)

    up_parcel, down_parcel = after((parcel(tiles - 1), parcel(0)), other)
    left_other, right_other = together(left_other, right_other)
    near[3] = jnp.concatenate([left_own, left_other], axis=0)
    near[1] = jnp.concatenate([right_own, right_other], axis=0)
    own_cot = scaled(cotangent, own_scales.reshape(local))
    places = jnp.stack(
        [
            (((x + r) % X) * YH + (yh + yr) % YH) * C + (c + cr) % C
            for r in range(X)
            for cr in range(C)
            for yr in range(YH)
        ]
    ).astype(jnp.int32)
    own_at = [k * tile for k in range(tiles)]
    rows_own, cot_own = by_distance(
        places, ([(tokens, k) for k in own_at], [(own_cot, k) for k in own_at]), tile
    )
    across[3] = core_swap(near[3])
    across[1] = core_swap(after(near[1], across[3]))
    half = YH * piece

    def span(r, cr):
        return slice((r * C + cr) * half, (r * C + cr + 1) * half)

    def projected(rows, cots, r, cr):
        weight = (across if cr else near)[r]
        return (
            dot(rows[:, span(r, cr)], weight[:, : 2 * hidden], 1, 0),
            dot(cots[:, span(r, cr)], weight[:, 2 * hidden :], 1, 0),
        )

    def total(rows, cots, group):
        parts = [projected(rows, cots, r, cr) for r in group for cr in range(C)]
        return sum(p[0] for p in parts), sum(p[1] for p in parts)

    early = total(rows_own, cot_own, (0, 3, 1))
    far_own, far_other, lower, upper, early = together(
        x_up(after(left_own, left_other)),
        x_down(right_other),
        blk_up(up_parcel),
        blk_down(down_parcel),
        early,
    )
    all_scales = jnp.concatenate(
        [own_scales.reshape(local), lower[2 * tile, :tile], upper[2 * tile, :tile]], axis=0
    )
    rows_vis, cot_vis = by_distance(
        places, ([(lower, 0), (upper, 0)], [(lower, tile), (upper, tile)]), tile
    )
    near[2] = jnp.concatenate([far_own, far_other], axis=0)
    across[2] = core_swap(near[2])
    early_vis = total(rows_vis, cot_vis, (0, 3, 1))
    stack = lambda a, b: jnp.concatenate([a, b], axis=0)
    rows, cots = stack(rows_own, rows_vis), stack(cot_own, cot_vis)
    late = total(rows, cots, (2,))
    gate_up = stack(early[0], early_vis[0]) + late[0]
    hidden_grad = stack(early[1], early_vis[1]) + late[1]
    gate_pre, up_pre = gate_up[:, :hidden], gate_up[:, hidden:]
    sig = jax.nn.sigmoid(gate_pre)
    act = gate_pre * sig
    hid = (act * up_pre).astype(BF)
    gate_grad = (hidden_grad * up_pre * sig * (1.0 + gate_pre * (1.0 - sig))).astype(BF)
    up_grad = (hidden_grad * act).astype(BF)
    both_grad = jnp.concatenate([gate_grad, up_grad], axis=1)

    sends, keeps = weight_grads(rows, cots, both_grad, hid, 2, 1, 1)
    came = core_swap(sends)
    sides_send, sides_keep = weight_grads(rows, cots, *after((both_grad, hid), sends), 1, 2, 2)
    came, sides_send = together(came, sides_send)
    far = (keeps + came.astype(F32)).astype(BF)
    far_a, far_b = x_up(far[:piece]), x_down(far[piece:])
    sides_came = core_swap(sides_send)

    late_hid, late_grad = after((hid, both_grad), sides_came)
    weights = [w for r in range(X) for w in (near[r], across[r])]
    own_out, own_grad, box_last, box_first = outputs_by_column(
        places, late_hid, late_grad, all_scales.astype(F32)[:, None], weights, local, tile
    )

    sends, keeps = weight_grads(rows, cots, late_grad, late_hid, 0, 1, 1)
    far_a, far_b, box_last, box_first, sends = together(
        far_a, far_b, box_last, box_first, sends
    )
    sides = sides_keep + sides_came.astype(F32)
    step_up = (sides[:half] + jnp.pad(far_a.astype(F32), ((0, piece), (0, 0)))).astype(BF)
    step_down = (sides[half:] + jnp.pad(far_b.astype(F32), ((piece, 0), (0, 0)))).astype(BF)
    come_up, come_down = x_up(step_up), x_down(step_down)
    back_last, back_first = blk_down(box_last), blk_up(box_first)
    came = core_swap(sends)
    summed = keeps + came.astype(F32) + come_up.astype(F32) + come_down.astype(F32)
    grads = summed[:piece] + yh_swap(summed[piece:].astype(BF)).astype(F32)
    merged, token_grad = settled(
        stay.astype(jnp.int32), own_out, own_grad, back_first, back_last, tile
    )
    return (
        merged,
        token_grad,
        grads[None, :, :hidden],
        grads[None, :, hidden : 2 * hidden],
        grads[None, :, 2 * hidden :],
    )


def solution(mesh):
    flat = P(("blk", "dp"))
    weight = P("blk", "dp", None)
    wide = P(("blk", "dp"), None)
    in_specs = (wide, wide, flat, flat, flat, weight, weight, weight)
    out_specs = (wide, wide, weight, weight, weight)
    return jax.shard_map(shards, mesh=mesh, in_specs=in_specs, out_specs=out_specs, check_vma=False)
```
